32 devices in a mesh: gx: 4 (over x, core), gy: 2 (over y), gz: 4 (over z).
Axes of the slice: x: 2, y: 2, z: 4, core: 2. Of those that a mesh axis runs over, the one named last changes fastest.
Arguments:
- tokens: bfloat16 [24, 6144], P(('gx', 'gy'), 'gz'), may hold values from -6 to 6
- w_up: bfloat16 [6144, 49152], P('gz', ('gx', 'gy')), may hold values from -0.078125 to 0.078125
- w_down: bfloat16 [49152, 6144], P(('gx', 'gy'), 'gz'), may hold values from -0.02734375 to 0.02734375
- cotangent: bfloat16 [24, 6144], P(('gx', 'gy'), 'gz'), may hold values from -6 to 6
Outputs:
- grad_in: float32 [24, 6144], P(('gx', 'gy'), 'gz')
- grad_up: bfloat16 [6144, 49152], P('gz', ('gx', 'gy'))
- grad_down: bfloat16 [49152, 6144], P(('gx', 'gy'), 'gz')
The draws below stay inside these ranges and needn't reach their ends.
All inputs are finite; a program needn't handle non-finite values.
Results may differ from the reference program's by a relative error of at most 0.0049.
Values may be sent and summed in bfloat16 or wider, within the bound.
No kernel may reach another device: no remote copies, remote signals or barrier semaphores. Data moves between devices by JAX's collectives and lax.ppermute only.
A program may use at most 128 MiB of HBM per device.

```python
import math
import jax
import jax.numpy as jnp

D = 6144
FF = 49152
TOKENS = 24


def level_of(rng, shape, split, least, high):
    factor_of, own = 1.0, jax.random.fold_in(rng, 6)
    for axis_at, blocks in split:
        steps = jnp.exp(jax.random.uniform(jax.random.fold_in(own, axis_at), (blocks,), jnp.float32, least / len(split), high / len(split)))
        factor_of = factor_of * jnp.repeat(steps, shape[axis_at] // blocks).reshape([-1 if axis == axis_at else 1 for axis in range(len(shape))])
    return factor_of


def noise(key, extent, spread, bound, cuts=(), dtype=jnp.bfloat16):
    array = spread * jax.random.normal(key, extent, jnp.float32)
    if cuts:
        array = array * level_of(key, extent, cuts, -0.22, 0.18)
    return jnp.clip(array, -bound, bound).astype(dtype)


def setup_inputs(seed: int = 0) -> dict:
    key_of = jax.random.split(jax.random.key(seed), 5)
    return {
        "tokens": noise(key_of[0], (TOKENS, D), 1.0, 6.0, ((0, 8), (1, 4))),
        "w_up": noise(key_of[1], (D, FF), D ** -0.5, 0.078125, ((0, 4), (1, 8))),
        "w_down": noise(key_of[2], (FF, D), FF ** -0.5, 0.02734375, ((0, 8), (1, 4))),
        "cotangent": noise(key_of[3], (TOKENS, D), 1.0, 6.0, ((0, 8), (1, 4))),
    }


GELU_SCALE = math.sqrt(2.0 / math.pi)
CUBIC_COEFF = 0.044715

def activate(pre_act, back_grad):
    squared = pre_act * pre_act
    tangent = jnp.tanh(GELU_SCALE * pre_act * (1.0 + CUBIC_COEFF * squared))
    hidden = (0.5 * pre_act * (1.0 + tangent)).astype(jnp.bfloat16)
    gelu_slope = 0.5 * (1.0 + tangent) + 0.5 * pre_act * (1.0 - tangent * tangent) * GELU_SCALE * (1.0 + 3.0 * CUBIC_COEFF * squared)
    return (hidden, (back_grad * gelu_slope).astype(jnp.bfloat16))

def reference(tokens, w_up, w_down, cotangent):
    pre_act = jnp.dot(tokens, w_up, preferred_element_type=jnp.float32)
    back_grad = jnp.dot(cotangent, w_down.T, preferred_element_type=jnp.float32)
    hidden, pre_grad = activate(pre_act, back_grad)
    grad_up = jnp.dot(tokens.T, pre_grad, preferred_element_type=jnp.float32).astype(jnp.bfloat16)
    grad_down = jnp.dot(hidden.T, cotangent, preferred_element_type=jnp.float32).astype(jnp.bfloat16)
    grad_in = jnp.dot(pre_grad, w_up.T, preferred_element_type=jnp.float32)
    return (grad_in, grad_up, grad_down)
```

```python
import functools
import math

import jax
import jax.numpy as jnp
from jax import lax
from jax.experimental import pallas as pl
from jax.experimental.pallas import tpu as pltpu
from jax.sharding import PartitionSpec as P

GELU_SCALE = math.sqrt(2.0 / math.pi)
CUBIC_COEFF = 0.044715
BF16 = jnp.bfloat16
F32 = jnp.float32
MIB = 1 << 20
PIECE = 512
SLAB = 256
STRIPES = 2
SMALL = 8 * MIB


def gelu(pre_act):
    squared = pre_act * pre_act
    tangent = jnp.tanh(GELU_SCALE * pre_act * (1.0 + CUBIC_COEFF * squared))
    hidden = (0.5 * pre_act * (1.0 + tangent)).astype(BF16)
    gelu_slope = 0.5 * (1.0 + tangent) + 0.5 * pre_act * (1.0 - tangent * tangent) * GELU_SCALE * (
        1.0 + 3.0 * CUBIC_COEFF * squared
    )
    return hidden, gelu_slope


def activate(pre_act, back_grad):
    hidden, gelu_slope = gelu(pre_act)
    return (hidden, (back_grad * gelu_slope).astype(BF16))


def plain(tokens, w_up, w_down, cotangent):
    rows_all, cot_all = (
        lax.all_gather(tokens, ("gx", "gy"), axis=0, tiled=True),
        lax.all_gather(cotangent, ("gx", "gy"), axis=0, tiled=True),
    )
    pre_part = jnp.dot(rows_all, w_up, preferred_element_type=F32)
    back_part = jnp.einsum("td,fd->tf", cot_all, w_down, preferred_element_type=F32)
    pre_act, back_grad = lax.psum((pre_part, back_part), "gz")
    hidden, pre_grad = activate(pre_act, back_grad)
    grad_up = jnp.einsum("td,tf->df", rows_all, pre_grad, preferred_element_type=F32).astype(BF16)
    grad_down = jnp.einsum("tf,td->fd", hidden, cot_all, preferred_element_type=F32).astype(BF16)
    grad_in = lax.psum_scatter(
        jnp.einsum("tf,df->td", pre_grad, w_up, preferred_element_type=F32),
        ("gx", "gy"),
        scatter_dimension=0,
        tiled=True,
    )
    return (grad_in, grad_up, grad_down)


def swap(value, axes, size, at):
    return lax.ppermute(value, axes, [(i, i ^ at) for i in range(size)])


def product(a, b, dims):
    return lax.dot_general(a, b, ((dims[:1], dims[1:]), ((), ())), preferred_element_type=F32)


def turn(block):
    return block.astype(F32).T.astype(BF16)


def in_vmem(count=1):
    return [pl.BlockSpec(memory_space=pltpu.VMEM)] * count


def anywhere(count=1):
    return [pl.BlockSpec(memory_space=pl.ANY)] * count


def keep_in(memory, value):
    return pltpu.with_memory_space_constraint(value, memory)


def cost(flops, bytes_accessed):
    return pl.CostEstimate(flops=flops, bytes_accessed=bytes_accessed, transcendentals=0)


def first_unit(other, quarter, size):
    return pl.multiple_of((((lax.axis_index("gz") & 1) ^ other) * 2 + quarter) * size, size)


def join_kernel(tokens_ref, cot_ref, out_ref, sems):
    copies = [
        pltpu.make_async_copy(from_ref, out_ref.at[i], sems.at[i]) for i, from_ref in enumerate((tokens_ref, cot_ref))
    ]
    for copy in copies:
        copy.start()
    for copy in copies:
        copy.wait()


def join(tokens, cotangent):
    return pl.pallas_call(
        join_kernel,
        in_specs=anywhere(2),
        out_specs=in_vmem()[0],
        out_shape=jax.ShapeDtypeStruct((2,) + tokens.shape, BF16),
        scratch_shapes=[pltpu.SemaphoreType.DMA((2,))],
        compiler_params=pltpu.CompilerParams(vmem_limit_bytes=SMALL),
        name="join",
    )(keep_in(pltpu.HBM, tokens), keep_in(pltpu.HBM, cotangent))


def pack_kernel(*refs):
    *block_refs, out_ref = refs
    for at, block_ref in enumerate(block_refs):
        out_ref[at] = block_ref[...]


def pack(blocks):
    return pl.pallas_call(
        pack_kernel,
        in_specs=in_vmem(len(blocks)),
        out_specs=in_vmem()[0],
        out_shape=jax.ShapeDtypeStruct((len(blocks),) + blocks[0].shape, BF16),
        compiler_params=pltpu.CompilerParams(vmem_limit_bytes=SMALL),
        name="pack",
    )(*blocks)


def unpack_kernel(*refs):
    *group_refs, rows_ref, cot_ref, turned_ref, wide = refs
    count, _, own, _ = group_refs[0].shape
    for i, out_ref in enumerate((rows_ref, cot_ref)):
        for to, (at, group_ref) in enumerate((at, x) for x in group_refs for at in range(count)):
            wide[i, to * own : (to + 1) * own] = group_ref[at, i].astype(F32)
        out_ref[...] = wide[i].astype(BF16)
    turned_ref[...] = turn(wide[0])


def unpack(groups):
    count, _, own, width = groups[0].shape
    tokens = own * count * len(groups)
    return pl.pallas_call(
        unpack_kernel,
        in_specs=in_vmem(len(groups)),
        out_specs=in_vmem(3),
        out_shape=[jax.ShapeDtypeStruct((tokens, width), BF16)] * 2 + [jax.ShapeDtypeStruct((width, tokens), BF16)],
        scratch_shapes=[pltpu.VMEM((2, tokens, width), F32)],
        compiler_params=pltpu.CompilerParams(vmem_limit_bytes=SMALL),
        name="unpack",
    )(*groups)


def add_up_kernel(*refs):
    *part_refs, out_ref = refs
    out_ref[...] = sum(part_ref[...].astype(F32) for part_ref in part_refs)


def add_up(parts):
    return pl.pallas_call(
        add_up_kernel,
        in_specs=in_vmem(len(parts)),
        out_specs=in_vmem()[0],
        out_shape=jax.ShapeDtypeStruct(parts[0].shape, F32),
        compiler_params=pltpu.CompilerParams(vmem_limit_bytes=SMALL),
        name="add_up",
    )(*parts)


class Copies:
    def __init__(self, from_ref, to_ref, sems):
        stripe = PIECE // STRIPES
        rows = [pl.ds(top, stripe) for top in range(0, to_ref.shape[0], stripe)]
        self.copies = [
            pltpu.make_async_copy(from_ref.at[at], to_ref.at[at], sems.at[i]) for i, at in enumerate(rows)
        ]

    def start(self):
        for copy in self.copies:
            copy.start()

    def wait(self):
        for copy in self.copies:
            copy.wait()


def up_copies(base, size, from_ref, to_ref, sems):
    columns, rows = pl.ds(base, size), range(0, to_ref.shape[0], PIECE)
    return [
        Copies(from_ref.at[pl.ds(top, PIECE), columns], to_ref.at[pl.ds(top, PIECE)], sems.at[i])
        for i, top in enumerate(rows)
    ]


def down_copies(base, size, from_ref, to_ref, sems):
    return [
        Copies(from_ref.at[pl.ds(base + top, PIECE)], to_ref.at[pl.ds(top, PIECE)], sems.at[i])
        for i, top in enumerate(range(0, size, PIECE))
    ]


def copy_sems(rows):
    return pltpu.SemaphoreType.DMA((rows // PIECE, STRIPES))


def load_kernel(other, quarter, up_ref, down_ref, _, up_kept, down_kept, up_sems, down_sems):
    size = up_kept.shape[1]
    base = first_unit(other, quarter, size)
    copies = up_copies(base, size, up_ref, up_kept, up_sems)
    copies += down_copies(base, size, down_ref, down_kept, down_sems)
    for copy in copies:
        copy.start()
    for copy in copies:
        copy.wait()


def load(w_up, w_down, other, quarter, after):
    width, units = w_up.shape
    size = units // 4
    return pl.pallas_call(
        functools.partial(load_kernel, other, quarter),
        in_specs=anywhere(3),
        out_specs=in_vmem(2),
        out_shape=[pltpu.VMEM((width, size), BF16), pltpu.VMEM((size, width), BF16)],
        scratch_shapes=[copy_sems(width), copy_sems(size)],
        compiler_params=pltpu.CompilerParams(vmem_limit_bytes=SMALL),
        cost_estimate=cost(0, 4 * width * size),
        name="load",
    )(keep_in(pltpu.HBM, w_up), keep_in(pltpu.HBM, w_down), after)


def multiply(rows_ref, cot_ref, up_buf, down_buf, out_ref, up_arriving=(), down_arriving=()):
    pre_act = None
    for i in range(up_buf.shape[0] // PIECE):
        piece = slice(i * PIECE, (i + 1) * PIECE)
        if up_arriving:
            up_arriving[i].wait()
        part = product(rows_ref[:, piece], up_buf[piece], (1, 0))
        pre_act = part if pre_act is None else pre_act + part
        if down_arriving:
            down_arriving[i].wait()
        out_ref[1, :, piece] = product(cot_ref[...], down_buf[piece], (1, 1)).astype(out_ref.dtype)
    out_ref[0] = pre_act.astype(out_ref.dtype)


def forward_other_kernel(rows_ref, cot_ref, up_first, down_first, up_ref, down_ref, *refs):
    first_out, second_out, up_kept, down_buf, *sems = refs
    size = up_kept.shape[1]
    base = first_unit(1, 1, size)
    ups = up_copies(base, size, up_ref, up_kept, sems[0])
    downs = down_copies(base, size, down_ref, down_buf, sems[1])
    for pair in zip(ups, downs):
        for copy in pair:
            copy.start()
    multiply(rows_ref, cot_ref, up_first, down_first, first_out)
    multiply(rows_ref, cot_ref, up_kept, down_buf, second_out, ups, downs)


def forward_other(rows, cot, up_first, down_first, w_up, w_down):
    tokens, width = rows.shape
    size = up_first.shape[1]
    return pl.pallas_call(
        forward_other_kernel,
        in_specs=in_vmem(4) + anywhere(2),
        out_specs=in_vmem(3),
        out_shape=[jax.ShapeDtypeStruct((2, tokens, size), BF16)] * 2 + [pltpu.VMEM((width, size), BF16)],
        scratch_shapes=[pltpu.VMEM((size, width), BF16), copy_sems(width), copy_sems(size)],
        compiler_params=pltpu.CompilerParams(vmem_limit_bytes=12 * MIB),
        cost_estimate=cost(8 * tokens * width * size, 4 * width * size),
        name="forward_other",
    )(
        rows,
        cot,
        keep_in(pltpu.VMEM, up_first),
        keep_in(pltpu.VMEM, down_first),
        keep_in(pltpu.HBM, w_up),
        keep_in(pltpu.HBM, w_down),
    )


def forward_own_kernel(quarter, rows_ref, cot_ref, up_ref, down_ref, *refs):
    out_ref, up_kept, down_buf, *sems = refs[-5:]
    size = up_kept.shape[1]
    base = first_unit(0, quarter, size)
    ups = up_copies(base, size, up_ref, up_kept, sems[0])
    downs = down_copies(base, size, down_ref, down_buf, sems[1])
    for pair in zip(ups, downs):
        for copy in pair:
            copy.start()
    multiply(rows_ref, cot_ref, up_kept, down_buf, out_ref, ups, downs)


def forward_own(rows, cot, w_up, w_down, quarter, after):
    tokens, width = rows.shape
    size = w_up.shape[1] // 4
    return pl.pallas_call(
        functools.partial(forward_own_kernel, quarter),
        in_specs=in_vmem(2) + anywhere(2 + len(after)),
        out_specs=in_vmem(2),
        out_shape=[jax.ShapeDtypeStruct((2, tokens, size), F32), pltpu.VMEM((width, size), BF16)],
        scratch_shapes=[pltpu.VMEM((size, width), BF16), copy_sems(width), copy_sems(size)],
        compiler_params=pltpu.CompilerParams(vmem_limit_bytes=12 * MIB),
        cost_estimate=cost(4 * tokens * width * size, 4 * width * size),
        name="forward_own",
    )(rows, cot, keep_in(pltpu.HBM, w_up), keep_in(pltpu.HBM, w_down), *after)


def activate_kernel(sums_ref, arrived_ref, *refs):
    sums = sums_ref[...] + arrived_ref[...].astype(F32)
    refs[-1][0], refs[-1][1] = activate(sums[0], sums[1])


def activated(sums, arrived, after):
    return pl.pallas_call(
        activate_kernel,
        in_specs=in_vmem(2) + anywhere(len(after)),
        out_specs=in_vmem()[0],
        out_shape=jax.ShapeDtypeStruct(sums.shape, BF16),
        compiler_params=pltpu.CompilerParams(vmem_limit_bytes=SMALL),
        name="activate",
    )(sums, arrived, *after)


def grad_in_sum(acts_ref, up_ref, turned):
    turned[...] = turn(acts_ref[1])
    return product(up_ref[...], turned[...], (1, 0)).T


def grads_kernel(places, shared, started, turned_ref, cot_ref, *refs):
    acts_refs, refs = refs[: len(places)], refs[len(places) :]
    up_refs, refs = refs[: len(places) * shared], refs[len(places) * shared :]
    again = shared and not started
    outs, scratch = refs[-8 - shared - again : -6], refs[-6:]
    up_out, down_out = outs[:2]
    if again:
        outs[3][...] = acts_refs[0][...]
    up_slots, down_slots, turned_hidden, turned_grad, up_sems, down_sems = scratch
    copies = []
    for place, (acts_ref, (other, quarter)) in enumerate(zip(acts_refs, places)):
        size = acts_ref.shape[2]
        base = first_unit(other, quarter, size)
        units = pl.ds(base, size)
        for i in range(size // SLAB):
            rows, slot = pl.ds(i * SLAB, SLAB), place * (size // SLAB) + i
            if i * SLAB % PIECE == 0:
                piece = slice(i * SLAB, i * SLAB + PIECE)
                turned_hidden[place, piece] = turn(acts_ref[0, :, piece])
            down_slots[slot] = product(turned_hidden[place, rows], cot_ref[...], (1, 0)).astype(BF16)
            to_ref = down_out.at[pl.ds(base + i * SLAB, SLAB)]
            copies.append(pltpu.make_async_copy(down_slots.at[slot], to_ref, down_sems.at[slot]))
            copies[-1].start()
        for i in range(turned_ref.shape[0] // SLAB):
            rows, slot = pl.ds(i * SLAB, SLAB), place * (turned_ref.shape[0] // SLAB) + i
            up_slots[slot] = product(turned_ref[rows], acts_ref[1], (1, 0)).astype(BF16)
            copies.append(pltpu.make_async_copy(up_slots.at[slot], up_out.at[rows, units], up_sems.at[slot]))
            copies[-1].start()
    if shared:
        total = refs[0][...] if started else None
        for place, (acts_ref, up_ref) in enumerate(zip(acts_refs, up_refs)):
            part = grad_in_sum(acts_ref, up_ref, turned_grad.at[place])
            total = part if total is None else total + part
        outs[2][...] = total
    for copy in copies:
        copy.wait()


def grads(turned, cot, units, places, acts, up_quarters=(), total=None, so_far=(), after=()):
    tokens, width = cot.shape
    size = acts[0].shape[2]
    ups, downs = (len(places) * x // SLAB for x in (width, size))
    shared = bool(up_quarters)
    totals = () if total is None else (total,)
    again = shared and not totals
    before = 2 + len(acts) + len(up_quarters) + len(totals)
    return pl.pallas_call(
        functools.partial(grads_kernel, places, shared, bool(totals)),
        in_specs=in_vmem(before) + anywhere(len(so_far) + len(after)),
        out_specs=anywhere(2) + in_vmem(shared + again),
        out_shape=[jax.ShapeDtypeStruct((width, units), BF16), jax.ShapeDtypeStruct((units, width), BF16)]
        + [jax.ShapeDtypeStruct((tokens, width), F32)] * shared
        + [jax.ShapeDtypeStruct(acts[0].shape, BF16)] * again,
        scratch_shapes=[
            pltpu.VMEM((ups, SLAB, size), BF16),
            pltpu.VMEM((downs, SLAB, width), BF16),
            pltpu.VMEM((len(places), size, tokens), BF16),
            pltpu.VMEM((len(places), size, tokens), BF16),
            pltpu.SemaphoreType.DMA((ups,)),
            pltpu.SemaphoreType.DMA((downs,)),
        ],
        input_output_aliases={before: 0, before + 1: 1} if so_far else {},
        compiler_params=pltpu.CompilerParams(vmem_limit_bytes=(4 + 12 * len(places)) * MIB),
        cost_estimate=cost(6 * tokens * width * size * len(places), 4 * width * size * len(places)),
        name="grads",
    )(turned, cot, *acts, *(keep_in(pltpu.VMEM, x) for x in up_quarters), *totals, *so_far, *after)


def grad_in_kernel(total_ref, acts_ref, up_ref, *out_refs):
    total = total_ref[...] + product(acts_ref[1], up_ref[...], (1, 1))
    count, own, _ = out_refs[0].shape
    for i in range(count * len(out_refs)):
        out_refs[i % len(out_refs)][i // len(out_refs)] = total[i * own : (i + 1) * own].astype(BF16)


def grad_in_parts(total, acts, up_quarter, cores, chips):
    tokens, width = total.shape
    size = acts.shape[2]
    return pl.pallas_call(
        grad_in_kernel,
        in_specs=in_vmem(3),
        out_specs=in_vmem(cores),
        out_shape=[jax.ShapeDtypeStruct((chips, tokens // chips // cores, width), BF16)] * cores,
        compiler_params=pltpu.CompilerParams(vmem_limit_bytes=SMALL),
        cost_estimate=cost(2 * tokens * width * size, 2 * width * size),
        name="grad_in",
    )(total, acts, keep_in(pltpu.VMEM, up_quarter))


def split_by_chip_kernel(*refs):
    chips = refs[0].shape[0]
    part_refs, out_refs = refs[:-chips], refs[-chips:]
    total = sum(part_ref[...].astype(F32) for part_ref in part_refs)
    for i, out_ref in enumerate(out_refs):
        out_ref[...] = total[i].astype(out_ref.dtype)


def split_by_chip(parts):
    chips, own, width = parts[0].shape
    return pl.pallas_call(
        split_by_chip_kernel,
        in_specs=in_vmem(len(parts)),
        out_specs=in_vmem(chips),
        out_shape=[jax.ShapeDtypeStruct((own, width), F32 if i == 0 else BF16) for i in range(chips)],
        compiler_params=pltpu.CompilerParams(vmem_limit_bytes=SMALL),
        name="split_by_chip",
    )(*parts)


def pair_sums_kernel(own_ref, arrived_ref, *refs):
    sums_ref, sent_ref = refs[-2:]
    sums = own_ref[...] + arrived_ref[...].astype(F32)
    sums_ref[...], sent_ref[...] = sums, sums.astype(BF16)


def pair_sums(own, arrived, after=()):
    return pl.pallas_call(
        pair_sums_kernel,
        in_specs=in_vmem(2) + anywhere(len(after)),
        out_specs=in_vmem(2),
        out_shape=[jax.ShapeDtypeStruct(own.shape, F32), jax.ShapeDtypeStruct(own.shape, BF16)],
        compiler_params=pltpu.CompilerParams(vmem_limit_bytes=SMALL),
        name="pair_sums",
    )(own, arrived, *after)


def split_plan(owners, splits, tokens, w_up, w_down, cotangent):
    group = ("gx", "gy")
    units = w_up.shape[1]
    core, chips = 2 % owners, [at for at in range(owners) if not at & 2]
    both = join(tokens, cotangent)
    both = pack([both, swap(both, group, owners, core)] if core else [both])
    kept, parts, sums, acts = {}, {}, {}, {}
    kept[1, 0], down_first = load(w_up, w_down, 1, 0, after=both)
    rows, cot, turned = unpack([both] + [swap(both, group, owners, at) for at in chips[1:]])

    parts[1, 0], parts[1, 1], kept[1, 1] = forward_other(rows, cot, kept[1, 0], down_first, w_up, w_down)
    theirs = [swap(parts[1, quarter], "gz", splits, 1) for quarter in (0, 1)]
    parts[0, 0], kept[0, 0] = forward_own(rows, cot, w_up, w_down, 0, after=(parts[1, 0],))
    sums[0], sent = pair_sums(parts[0, 0], theirs[0])
    arrived = swap(sent, "gz", splits, 2)
    parts[0, 1], kept[0, 1] = forward_own(rows, cot, w_up, w_down, 1, after=(sent, theirs[1]))
    sums[1], sent = pair_sums(parts[0, 1], theirs[1])
    late = swap(sent, "gz", splits, 2)

    acts[0, 0] = activated(sums[0], arrived, after=(sent,))
    *grad_arrays, total, again = grads(turned, cot, units, [(0, 0)], [acts[0, 0]], [kept[0, 0]])
    acts[1, 0] = swap(again, "gz", splits, 1)
    acts[0, 1] = activated(sums[1], late, after=(total,))
    acts[1, 1] = swap(acts[0, 1], "gz", splits, 1)
    for place in [(0, 1), (1, 0)]:
        *grad_arrays, total = grads(turned, cot, units, [place], [acts[place]], [kept[place]], total, grad_arrays)
    by_core = grad_in_parts(total, acts[1, 1], kept[1, 1], 2 if core else 1, len(chips))
    by_core = [by_core[0]] + [swap(x, group, owners, core) for x in by_core[1:]]
    by_chip = split_by_chip(by_core)
    grad_up, grad_down = grads(
        turned, cot, units, [(1, 1)], [acts[1, 1]], so_far=grad_arrays, after=(by_chip[0],)
    )
    grad_in = add_up([by_chip[0]] + [swap(x, group, owners, at) for x, at in zip(by_chip[1:], chips[1:])])
    return (grad_in, grad_up, grad_down)


def solution(mesh):
    owners, splits = mesh.shape["gx"] * mesh.shape["gy"], mesh.shape["gz"]

    def on_device(tokens, w_up, w_down, cotangent):
        if w_up.shape[1] % (4 * PIECE) or w_up.shape[0] % PIECE or owners > 8 or splits != 4:
            return plain(tokens, w_up, w_down, cotangent)
        return split_plan(owners, splits, tokens, w_up, w_down, cotangent)

    placed = (
        P(("gx", "gy"), "gz"),
        P("gz", ("gx", "gy")),
        P(("gx", "gy"), "gz"),
        P(("gx", "gy"), "gz"),
    )
    return jax.shard_map(
        on_device,
        mesh=mesh,
        in_specs=placed,
        out_specs=(P(("gx", "gy"), "gz"), P("gz", ("gx", "gy")), P(("gx", "gy"), "gz")),
        check_vma=False,
    )
```

```python
import functools
import math

import jax
import jax.numpy as jnp
from jax import lax
from jax.experimental import pallas as pl
from jax.experimental.pallas import tpu as pltpu
from jax.sharding import PartitionSpec as P

GELU_SCALE = math.sqrt(2.0 / math.pi)
CUBIC_COEFF = 0.044715
BF16 = jnp.bfloat16
F32 = jnp.float32
MIB = 1 << 20
PIECE = 512
SLAB = 256
STRIPES = 2
SMALL = 8 * MIB


def gelu(pre_act):
    squared = pre_act * pre_act
    tangent = jnp.tanh(GELU_SCALE * pre_act * (1.0 + CUBIC_COEFF * squared))
    hidden = (0.5 * pre_act * (1.0 + tangent)).astype(BF16)
    gelu_slope = 0.5 * (1.0 + tangent) + 0.5 * pre_act * (1.0 - tangent * tangent) * GELU_SCALE * (
        1.0 + 3.0 * CUBIC_COEFF * squared
    )
    return hidden, gelu_slope


def activate(pre_act, back_grad):
    hidden, gelu_slope = gelu(pre_act)
    return (hidden, (back_grad * gelu_slope).astype(BF16))


def plain(tokens, w_up, w_down, cotangent):
    rows_all, cot_all = (
        lax.all_gather(tokens, ("gx", "gy"), axis=0, tiled=True),
        lax.all_gather(cotangent, ("gx", "gy"), axis=0, tiled=True),
    )
    pre_part = jnp.dot(rows_all, w_up, preferred_element_type=F32)
    back_part = jnp.einsum("td,fd->tf", cot_all, w_down, preferred_element_type=F32)
    pre_act, back_grad = lax.psum((pre_part, back_part), "gz")
    hidden, pre_grad = activate(pre_act, back_grad)
    grad_up = jnp.einsum("td,tf->df", rows_all, pre_grad, preferred_element_type=F32).astype(BF16)
    grad_down = jnp.einsum("tf,td->fd", hidden, cot_all, preferred_element_type=F32).astype(BF16)
    grad_in = lax.psum_scatter(
        jnp.einsum("tf,df->td", pre_grad, w_up, preferred_element_type=F32),
        ("gx", "gy"),
        scatter_dimension=0,
        tiled=True,
    )
    return (grad_in, grad_up, grad_down)


def swap(value, axes, size, at):
    return lax.ppermute(value, axes, [(i, i ^ at) for i in range(size)])


def product(a, b, dims):
    return lax.dot_general(a, b, ((dims[:1], dims[1:]), ((), ())), preferred_element_type=F32)


def turn(block):
    return block.astype(F32).T.astype(BF16)


def in_vmem(count=1):
    return [pl.BlockSpec(memory_space=pltpu.VMEM)] * count


def anywhere(count=1):
    return [pl.BlockSpec(memory_space=pl.ANY)] * count


def keep_in(memory, value):
    return pltpu.with_memory_space_constraint(value, memory)


def cost(flops, bytes_accessed):
    return pl.CostEstimate(flops=flops, bytes_accessed=bytes_accessed, transcendentals=0)


def first_unit(other, quarter, size):
    return pl.multiple_of((((lax.axis_index("gz") & 1) ^ other) * 2 + quarter) * size, size)


def join_kernel(tokens_ref, cot_ref, out_ref, sems):
    copies = [
        pltpu.make_async_copy(from_ref, out_ref.at[i], sems.at[i]) for i, from_ref in enumerate((tokens_ref, cot_ref))
    ]
    for copy in copies:
        copy.start()
    for copy in copies:
        copy.wait()


def join(tokens, cotangent):
    return pl.pallas_call(
        join_kernel,
        in_specs=anywhere(2),
        out_specs=in_vmem()[0],
        out_shape=jax.ShapeDtypeStruct((2,) + tokens.shape, BF16),
        scratch_shapes=[pltpu.SemaphoreType.DMA((2,))],
        compiler_params=pltpu.CompilerParams(vmem_limit_bytes=SMALL),
        name="join",
    )(keep_in(pltpu.HBM, tokens), keep_in(pltpu.HBM, cotangent))


def pack_kernel(*refs):
    *block_refs, out_ref = refs
    for at, block_ref in enumerate(block_refs):
        out_ref[at] = block_ref[...]


def pack(blocks):
    return pl.pallas_call(
        pack_kernel,
        in_specs=in_vmem(len(blocks)),
        out_specs=in_vmem()[0],
        out_shape=jax.ShapeDtypeStruct((len(blocks),) + blocks[0].shape, BF16),
        compiler_params=pltpu.CompilerParams(vmem_limit_bytes=SMALL),
        name="pack",
    )(*blocks)


def unpack_kernel(*refs):
    *group_refs, rows_ref, cot_ref, turned_ref, wide = refs
    count, _, own, _ = group_refs[0].shape
    for i, out_ref in enumerate((rows_ref, cot_ref)):
        for to, (at, group_ref) in enumerate((at, x) for x in group_refs for at in range(count)):
            wide[i, to * own : (to + 1) * own] = group_ref[at, i].astype(F32)
        out_ref[...] = wide[i].astype(BF16)
    turned_ref[...] = turn(wide[0])


def unpack(groups):
    count, _, own, width = groups[0].shape
    tokens = own * count * len(groups)
    return pl.pallas_call(
        unpack_kernel,
        in_specs=in_vmem(len(groups)),
        out_specs=in_vmem(3),
        out_shape=[jax.ShapeDtypeStruct((tokens, width), BF16)] * 2 + [jax.ShapeDtypeStruct((width, tokens), BF16)],
        scratch_shapes=[pltpu.VMEM((2, tokens, width), F32)],
        compiler_params=pltpu.CompilerParams(vmem_limit_bytes=SMALL),
        name="unpack",
    )(*groups)


def add_up_kernel(*refs):
    *part_refs, out_ref = refs
    out_ref[...] = sum(part_ref[...].astype(F32) for part_ref in part_refs)


def add_up(parts):
    return pl.pallas_call(
        add_up_kernel,
        in_specs=in_vmem(len(parts)),
        out_specs=in_vmem()[0],
        out_shape=jax.ShapeDtypeStruct(parts[0].shape, F32),
        compiler_params=pltpu.CompilerParams(vmem_limit_bytes=SMALL),
        name="add_up",
    )(*parts)


class Copies:
    def __init__(self, from_ref, to_ref, sems):
        stripe = PIECE // STRIPES
        rows = [pl.ds(top, stripe) for top in range(0, to_ref.shape[0], stripe)]
        self.copies = [
            pltpu.make_async_copy(from_ref.at[at], to_ref.at[at], sems.at[i]) for i, at in enumerate(rows)
        ]

    def start(self):
        for copy in self.copies:
            copy.start()

    def wait(self):
        for copy in self.copies:
            copy.wait()


def up_copies(base, size, from_ref, to_ref, sems):
    columns, rows = pl.ds(base, size), range(0, to_ref.shape[0], PIECE)
    return [
        Copies(from_ref.at[pl.ds(top, PIECE), columns], to_ref.at[pl.ds(top, PIECE)], sems.at[i])
        for i, top in enumerate(rows)
    ]


def down_copies(base, size, from_ref, to_ref, sems):
    return [
        Copies(from_ref.at[pl.ds(base + top, PIECE)], to_ref.at[pl.ds(top, PIECE)], sems.at[i])
        for i, top in enumerate(range(0, size, PIECE))
    ]


def copy_sems(rows):
    return pltpu.SemaphoreType.DMA((rows // PIECE, STRIPES))


def load_kernel(up_ref, down_ref, _, *refs):
    *up_kept, down_kept, first_sems, second_sems, down_sems = refs
    size = down_kept.shape[0]
    copies = up_copies(first_unit(1, 0, size), size, up_ref, up_kept[0], first_sems)
    copies += down_copies(first_unit(1, 0, size), size, down_ref, down_kept, down_sems)
    copies += up_copies(first_unit(1, 1, size), size, up_ref, up_kept[1], second_sems)
    for copy in copies:
        copy.start()
    for copy in copies:
        copy.wait()


def load(w_up, w_down, after):
    width, units = w_up.shape
    size = units // 4
    return pl.pallas_call(
        load_kernel,
        in_specs=anywhere(3),
        out_specs=in_vmem(3),
        out_shape=[pltpu.VMEM((width, size), BF16)] * 2 + [pltpu.VMEM((size, width), BF16)],
        scratch_shapes=[copy_sems(width), copy_sems(width), copy_sems(size)],
        compiler_params=pltpu.CompilerParams(vmem_limit_bytes=SMALL),
        cost_estimate=cost(0, 6 * width * size),
        name="load",
    )(keep_in(pltpu.HBM, w_up), keep_in(pltpu.HBM, w_down), after)


def multiply(rows_ref, cot_ref, up_buf, down_buf, out_ref, up_arriving=(), down_arriving=()):
    pre_act = None
    for i in range(up_buf.shape[0] // PIECE):
        piece = slice(i * PIECE, (i + 1) * PIECE)
        if up_arriving:
            up_arriving[i].wait()
        part = product(rows_ref[:, piece], up_buf[piece], (1, 0))
        pre_act = part if pre_act is None else pre_act + part
        if down_arriving:
            down_arriving[i].wait()
        out_ref[1, :, piece] = product(cot_ref[...], down_buf[piece], (1, 1)).astype(out_ref.dtype)
    out_ref[0] = pre_act.astype(out_ref.dtype)


def forward_other_kernel(rows_ref, cot_ref, up_first, up_second, down_first, down_ref, *refs):
    first_out, second_out, down_buf, sems = refs
    size = down_buf.shape[0]
    downs = down_copies(first_unit(1, 1, size), size, down_ref, down_buf, sems)
    for copy in downs:
        copy.start()
    multiply(rows_ref, cot_ref, up_first, down_first, first_out)
    multiply(rows_ref, cot_ref, up_second, down_buf, second_out, (), downs)


def forward_other(rows, cot, up_first, up_second, down_first, w_down):
    tokens, width = rows.shape
    size = up_first.shape[1]
    kept = (keep_in(pltpu.VMEM, x) for x in (up_first, up_second, down_first))
    return pl.pallas_call(
        forward_other_kernel,
        in_specs=in_vmem(5) + anywhere(),
        out_specs=in_vmem(2),
        out_shape=[jax.ShapeDtypeStruct((2, tokens, size), BF16)] * 2,
        scratch_shapes=[pltpu.VMEM((size, width), BF16), copy_sems(size)],
        compiler_params=pltpu.CompilerParams(vmem_limit_bytes=12 * MIB),
        cost_estimate=cost(8 * tokens * width * size, 2 * width * size),
        name="forward_other",
    )(rows, cot, *kept, keep_in(pltpu.HBM, w_down))


def forward_own_kernel(quarter, rows_ref, cot_ref, up_ref, down_ref, *refs):
    out_ref, up_kept, down_buf, *sems = refs[-5:]
    size = up_kept.shape[1]
    base = first_unit(0, quarter, size)
    ups = up_copies(base, size, up_ref, up_kept, sems[0])
    downs = down_copies(base, size, down_ref, down_buf, sems[1])
    for pair in zip(ups, downs):
        for copy in pair:
            copy.start()
    multiply(rows_ref, cot_ref, up_kept, down_buf, out_ref, ups, downs)


def forward_own(rows, cot, w_up, w_down, quarter, after):
    tokens, width = rows.shape
    size = w_up.shape[1] // 4
    return pl.pallas_call(
        functools.partial(forward_own_kernel, quarter),
        in_specs=in_vmem(2) + anywhere(2 + len(after)),
        out_specs=in_vmem(2),
        out_shape=[jax.ShapeDtypeStruct((2, tokens, size), F32), pltpu.VMEM((width, size), BF16)],
        scratch_shapes=[pltpu.VMEM((size, width), BF16), copy_sems(width), copy_sems(size)],
        compiler_params=pltpu.CompilerParams(vmem_limit_bytes=12 * MIB),
        cost_estimate=cost(4 * tokens * width * size, 4 * width * size),
        name="forward_own",
    )(rows, cot, keep_in(pltpu.HBM, w_up), keep_in(pltpu.HBM, w_down), *after)


def activate_kernel(sums_ref, arrived_ref, *refs):
    sums = sums_ref[...] + arrived_ref[...].astype(F32)
    refs[-1][0], refs[-1][1] = activate(sums[0], sums[1])


def activated(sums, arrived, after):
    return pl.pallas_call(
        activate_kernel,
        in_specs=in_vmem(2) + anywhere(len(after)),
        out_specs=in_vmem()[0],
        out_shape=jax.ShapeDtypeStruct(sums.shape, BF16),
        compiler_params=pltpu.CompilerParams(vmem_limit_bytes=SMALL),
        name="activate",
    )(sums, arrived, *after)


def grad_in_sum(acts_ref, up_ref, turned):
    turned[...] = turn(acts_ref[1])
    return product(up_ref[...], turned[...], (1, 0)).T


def grads_kernel(places, shared, started, turned_ref, cot_ref, *refs):
    acts_refs, refs = refs[: len(places)], refs[len(places) :]
    up_refs, refs = refs[: len(places) * shared], refs[len(places) * shared :]
    again = shared and not started
    outs, scratch = refs[-8 - shared - again : -6], refs[-6:]
    up_out, down_out = outs[:2]
    if again:
        outs[3][...] = acts_refs[0][...]
    up_slots, down_slots, turned_hidden, turned_grad, up_sems, down_sems = scratch
    copies = []
    for place, (acts_ref, (other, quarter)) in enumerate(zip(acts_refs, places)):
        size = acts_ref.shape[2]
        base = first_unit(other, quarter, size)
        units = pl.ds(base, size)
        for i in range(size // SLAB):
            rows, slot = pl.ds(i * SLAB, SLAB), place * (size // SLAB) + i
            if i * SLAB % PIECE == 0:
                piece = slice(i * SLAB, i * SLAB + PIECE)
                turned_hidden[place, piece] = turn(acts_ref[0, :, piece])
            down_slots[slot] = product(turned_hidden[place, rows], cot_ref[...], (1, 0)).astype(BF16)
            to_ref = down_out.at[pl.ds(base + i * SLAB, SLAB)]
            copies.append(pltpu.make_async_copy(down_slots.at[slot], to_ref, down_sems.at[slot]))
            copies[-1].start()
        for i in range(turned_ref.shape[0] // SLAB):
            rows, slot = pl.ds(i * SLAB, SLAB), place * (turned_ref.shape[0] // SLAB) + i
            up_slots[slot] = product(turned_ref[rows], acts_ref[1], (1, 0)).astype(BF16)
            copies.append(pltpu.make_async_copy(up_slots.at[slot], up_out.at[rows, units], up_sems.at[slot]))
            copies[-1].start()
    if shared:
        total = refs[0][...] if started else None
        for place, (acts_ref, up_ref) in enumerate(zip(acts_refs, up_refs)):
            part = grad_in_sum(acts_ref, up_ref, turned_grad.at[place])
            total = part if total is None else total + part
        outs[2][...] = total
    for copy in copies:
        copy.wait()


def grads(turned, cot, units, places, acts, up_quarters=(), total=None, so_far=(), after=()):
    tokens, width = cot.shape
    size = acts[0].shape[2]
    ups, downs = (len(places) * x // SLAB for x in (width, size))
    shared = bool(up_quarters)
    totals = () if total is None else (total,)
    again = shared and not totals
    before = 2 + len(acts) + len(up_quarters) + len(totals)
    return pl.pallas_call(
        functools.partial(grads_kernel, places, shared, bool(totals)),
        in_specs=in_vmem(before) + anywhere(len(so_far) + len(after)),
        out_specs=anywhere(2) + in_vmem(shared + again),
        out_shape=[jax.ShapeDtypeStruct((width, units), BF16), jax.ShapeDtypeStruct((units, width), BF16)]
        + [jax.ShapeDtypeStruct((tokens, width), F32)] * shared
        + [jax.ShapeDtypeStruct(acts[0].shape, BF16)] * again,
        scratch_shapes=[
            pltpu.VMEM((ups, SLAB, size), BF16),
            pltpu.VMEM((downs, SLAB, width), BF16),
            pltpu.VMEM((len(places), size, tokens), BF16),
            pltpu.VMEM((len(places), size, tokens), BF16),
            pltpu.SemaphoreType.DMA((ups,)),
            pltpu.SemaphoreType.DMA((downs,)),
        ],
        input_output_aliases={before: 0, before + 1: 1} if so_far else {},
        compiler_params=pltpu.CompilerParams(vmem_limit_bytes=(4 + 12 * len(places)) * MIB),
        cost_estimate=cost(6 * tokens * width * size * len(places), 4 * width * size * len(places)),
        name="grads",
    )(turned, cot, *acts, *(keep_in(pltpu.VMEM, x) for x in up_quarters), *totals, *so_far, *after)


def grad_in_kernel(total_ref, acts_ref, up_ref, *out_refs):
    total = total_ref[...] + product(acts_ref[1], up_ref[...], (1, 1))
    count, own, _ = out_refs[0].shape
    for i in range(count * len(out_refs)):
        out_refs[i % len(out_refs)][i // len(out_refs)] = total[i * own : (i + 1) * own].astype(BF16)


def grad_in_parts(total, acts, up_quarter, cores, chips):
    tokens, width = total.shape
    size = acts.shape[2]
    return pl.pallas_call(
        grad_in_kernel,
        in_specs=in_vmem(3),
        out_specs=in_vmem(cores),
        out_shape=[jax.ShapeDtypeStruct((chips, tokens // chips // cores, width), BF16)] * cores,
        compiler_params=pltpu.CompilerParams(vmem_limit_bytes=SMALL),
        cost_estimate=cost(2 * tokens * width * size, 2 * width * size),
        name="grad_in",
    )(total, acts, keep_in(pltpu.VMEM, up_quarter))


def split_by_chip_kernel(*refs):
    chips = refs[0].shape[0]
    part_refs, out_refs = refs[:-chips], refs[-chips:]
    total = sum(part_ref[...].astype(F32) for part_ref in part_refs)
    for i, out_ref in enumerate(out_refs):
        out_ref[...] = total[i].astype(out_ref.dtype)


def split_by_chip(parts):
    chips, own, width = parts[0].shape
    return pl.pallas_call(
        split_by_chip_kernel,
        in_specs=in_vmem(len(parts)),
        out_specs=in_vmem(chips),
        out_shape=[jax.ShapeDtypeStruct((own, width), F32 if i == 0 else BF16) for i in range(chips)],
        compiler_params=pltpu.CompilerParams(vmem_limit_bytes=SMALL),
        name="split_by_chip",
    )(*parts)


def pair_sums_kernel(own_ref, arrived_ref, *refs):
    sums_ref, sent_ref = refs[-2:]
    sums = own_ref[...] + arrived_ref[...].astype(F32)
    sums_ref[...], sent_ref[...] = sums, sums.astype(BF16)


def pair_sums(own, arrived, after=()):
    return pl.pallas_call(
        pair_sums_kernel,
        in_specs=in_vmem(2) + anywhere(len(after)),
        out_specs=in_vmem(2),
        out_shape=[jax.ShapeDtypeStruct(own.shape, F32), jax.ShapeDtypeStruct(own.shape, BF16)],
        compiler_params=pltpu.CompilerParams(vmem_limit_bytes=SMALL),
        name="pair_sums",
    )(own, arrived, *after)


def split_plan(owners, splits, tokens, w_up, w_down, cotangent):
    group = ("gx", "gy")
    units = w_up.shape[1]
    core, chips = 2 % owners, [at for at in range(owners) if not at & 2]
    both = join(tokens, cotangent)
    both = pack([both, swap(both, group, owners, core)] if core else [both])
    kept, parts, sums, acts = {}, {}, {}, {}
    kept[1, 0], kept[1, 1], down_first = load(w_up, w_down, after=both)
    rows, cot, turned = unpack([both] + [swap(both, group, owners, at) for at in chips[1:]])

    parts[1, 0], parts[1, 1] = forward_other(rows, cot, kept[1, 0], kept[1, 1], down_first, w_down)
    theirs = [swap(parts[1, quarter], "gz", splits, 1) for quarter in (0, 1)]
    parts[0, 0], kept[0, 0] = forward_own(rows, cot, w_up, w_down, 0, after=(parts[1, 0],))
    sums[0], sent = pair_sums(parts[0, 0], theirs[0])
    arrived = swap(sent, "gz", splits, 2)
    parts[0, 1], kept[0, 1] = forward_own(rows, cot, w_up, w_down, 1, after=(sent, theirs[1]))
    sums[1], sent = pair_sums(parts[0, 1], theirs[1])
    late = swap(sent, "gz", splits, 2)

    acts[0, 0] = activated(sums[0], arrived, after=(sent,))
    *grad_arrays, total, again = grads(turned, cot, units, [(0, 0)], [acts[0, 0]], [kept[0, 0]])
    acts[1, 0] = swap(again, "gz", splits, 1)
    acts[0, 1] = activated(sums[1], late, after=(total,))
    acts[1, 1] = swap(acts[0, 1], "gz", splits, 1)
    for place in [(0, 1), (1, 0)]:
        *grad_arrays, total = grads(turned, cot, units, [place], [acts[place]], [kept[place]], total, grad_arrays)
    by_core = grad_in_parts(total, acts[1, 1], kept[1, 1], 2 if core else 1, len(chips))
    by_core = [by_core[0]] + [swap(x, group, owners, core) for x in by_core[1:]]
    by_chip = split_by_chip(by_core)
    grad_up, grad_down = grads(
        turned, cot, units, [(1, 1)], [acts[1, 1]], so_far=grad_arrays, after=(by_chip[0],)
    )
    grad_in = add_up([by_chip[0]] + [swap(x, group, owners, at) for x, at in zip(by_chip[1:], chips[1:])])
    return (grad_in, grad_up, grad_down)


def solution(mesh):
    owners, splits = mesh.shape["gx"] * mesh.shape["gy"], mesh.shape["gz"]

    def on_device(tokens, w_up, w_down, cotangent):
        if w_up.shape[1] % (4 * PIECE) or w_up.shape[0] % PIECE or owners > 8 or splits != 4:
            return plain(tokens, w_up, w_down, cotangent)
        return split_plan(owners, splits, tokens, w_up, w_down, cotangent)

    placed = (
        P(("gx", "gy"), "gz"),
        P("gz", ("gx", "gy")),
        P(("gx", "gy"), "gz"),
        P(("gx", "gy"), "gz"),
    )
    return jax.shard_map(
        on_device,
        mesh=mesh,
        in_specs=placed,
        out_specs=(P(("gx", "gy"), "gz"), P("gz", ("gx", "gy")), P(("gx", "gy"), "gz")),
        check_vma=False,
    )
```
